32 devices in a mesh: groups: 2 (over x), expert: 16 (over z, y, core).
Axes of the slice: x: 2, y: 2, z: 4, core: 2. Of those that a mesh axis runs over, the one named last changes fastest.
Arguments:
- tokens: bfloat16 [1024, 2048], P(('groups', 'expert')), parts along dimension 0, may hold values from -6 to 6
- out_grad: bfloat16 [1024, 2048], P(('groups', 'expert')), parts along dimension 0, may hold values from -6 to 6
- routes: int32 [1024, 8], P(('groups', 'expert')), parts along dimension 0, may hold values from 0 to 15, all different within a row; in each aligned block of 32 rows (0 to 31, 32 to 63, ...) at most 32 rows name the same one
- probs: bfloat16 [1024, 8], P(('groups', 'expert')), parts along dimension 0, may hold values from 0.019897461 to 0.29882812
- w_gate: bfloat16 [16, 2048, 768], P('expert'), may hold values from -0.125 to 0.125
- w_up: bfloat16 [16, 2048, 768], P('expert'), may hold values from -0.125 to 0.125
- w_down: bfloat16 [16, 768, 2048], P('expert'), may hold values from -0.21875 to 0.21875
Outputs:
- input_grad: bfloat16 [1024, 2048], P(('groups', 'expert')), parts along dimension 0
- prob_grad: bfloat16 [1024, 8], P(('groups', 'expert')), parts along dimension 0
- down_grad: bfloat16 [32, 768, 2048], P(('groups', 'expert')), parts along dimension 0
The draws below stay inside these ranges and needn't reach their ends.
There are 2 independent parts, one for each index of `groups`. The reference program is written for one: setup_inputs(seed, part) draws one part's arguments, and reference() takes and returns one part's arrays. A program takes and returns all parts, laid end to end along the dimension named above; an argument that names none is the same for every part. Nothing has to cross between parts.
Inputs may be any that keep to these rules, and one draw needn't show every extreme that they name: `routes`: each token names 8 different experts. Among the tokens of one device no expert is named more than 32 times, a bound that some block reaches.
All inputs are finite; a program needn't handle non-finite values.
Results may differ from the reference program's by a relative error of at most 0.0057.
Values may be sent and summed in bfloat16 or wider, within the bound.
A program may use at most 64 MiB of HBM per device.

```python
import math
import jax
import jax.numpy as jnp
import numpy as np
from jax import lax

D = 2048
FF = 768
TOPK = 8
TOK_DEV = 32
EXPERTS = 16
SLOT = 32
TOKENS = 512
N_EXPERT = 16


def block_scale(rng, shape, cuts, low, top_value):
    loudness = 1.0
    for position, parts in cuts:
        draws = jax.random.uniform(jax.random.fold_in(jax.random.fold_in(rng, 6), position), (parts,), jnp.float32, low / len(cuts), top_value / len(cuts))
        loudness = loudness * jnp.repeat(jnp.exp(draws), shape[position] // parts).reshape((-1,) + (1,) * (len(shape) - 1 - position))
    return loudness


def assign_block(key, own, number, rows, number_of, top, reach, slope):
    sequence = jax.random.permutation(key, number_of)
    packed, common = load_shares(number_of, rows * top, reach, slope, True), load_shares(number_of, rows * top, reach, slope, False)
    places = jnp.arange(number_of)

    def named(lengths, turn):
        used = int((lengths > 0).sum())
        fixed = max(1, used // 4)
        shifted = fixed + (places - fixed + turn * (used - fixed)) % max(1, number_of - fixed)
        return jnp.zeros((number_of,), jnp.int32).at[sequence[jnp.where(places < fixed, places, shifted)]].set(jnp.asarray(lengths, jnp.int32))

    lengths = jnp.where(number % 4 == 0, named(packed, number // 4), named(common, number - number // 4 - 1))
    mixed = jax.random.permutation(jax.random.fold_in(own, 3), number_of)
    giver, sink = mixed[0:number_of // 2 * 2:2], mixed[1:number_of // 2 * 2:2]
    slack = jnp.minimum(lengths[giver] - 1, reach - lengths[sink]) // 2
    slack = jnp.where((giver == sequence[0]) | (sink == sequence[0]) | (lengths[sink] == 0), 0, jnp.maximum(slack, 0))
    shifted = jax.random.randint(jax.random.fold_in(own, 4), (number_of // 2,), 0, 1 << 20) % (slack + 1)
    lengths = lengths.at[giver].add(-shifted).at[sink].add(shifted)
    labels = jnp.searchsorted(jnp.cumsum(lengths), jnp.arange(rows * top), side="right").astype(jnp.int32)
    grid = labels.reshape(top, rows).T
    grid = grid[jax.random.permutation(jax.random.fold_in(own, 1), rows)]
    turn = jax.random.randint(jax.random.fold_in(own, 2), (rows, 1), 0, top)
    return jnp.take_along_axis(grid, (jnp.arange(top)[None, :] + turn) % top, axis=1)


def load_shares(amount, total, most, skew, full):
    weights = [(1 << 20) // math.isqrt(grade ** skew) + 1 for grade in range(1, amount + 1)]
    largest = most if full else min(most, max(-(-total // amount), total * weights[0] // sum(weights)))
    least = 1 if total - largest >= amount - 1 else 0
    counts, surplus = [largest] + [least] * (amount - 1), total - largest - least * (amount - 1)
    while surplus > 0:
        candidates = [i for i in range(1, amount) if counts[i] < largest] or [i for i in range(1, amount) if counts[i] < most]
        whole, remaining = sum([weights[i] for i in candidates]), surplus
        for i in candidates:
            extra = min(most - counts[i], max(1, remaining * weights[i] // whole), surplus)
            counts[i] = counts[i] + extra
            surplus = surplus - extra
    return np.array(counts)


def noise(key, shape, width, limit, split=(), kind=jnp.bfloat16):
    array = jax.random.normal(key, shape, jnp.float32) * width
    if len(split) > 0:
        array = block_scale(key, shape, split, -0.22, 0.18) * array
    return jnp.clip(array, min=-limit, max=limit).astype(kind)


def setup_inputs(seed: int = 0, part: int = 0) -> dict:
    splits = jax.random.split(jax.random.key(seed), 8)
    part_keys = jax.random.split(jax.random.fold_in(splits[7], part), 8)
    tokens = noise(part_keys[0], (TOKENS, D), 1.0, 6.0, ((0, 16),))
    out_grad = noise(part_keys[1], (TOKENS, D), 1.0, 6.0, ((0, 16),))
    routes_keys = jax.random.split(jax.random.fold_in(part_keys[2], 1), TOKENS // TOK_DEV)
    routes_turns = jax.random.permutation(jax.random.fold_in(part_keys[2], 3), TOKENS // TOK_DEV)
    routes = jax.vmap(lambda own, number: assign_block(jax.random.fold_in(part_keys[2], 2), own, number, TOK_DEV, EXPERTS, TOPK, SLOT, 2))(routes_keys, routes_turns).reshape((TOKENS, TOPK))
    probs = jnp.clip(0.019897461 + 0.27893066 * jax.random.uniform(part_keys[3], (TOKENS, TOPK), jnp.float32) ** block_scale(part_keys[3], (TOKENS, TOPK), ((0, 16),), -0.2, 0.2), 0.019897461, 0.29882812).astype(jnp.bfloat16)
    w_gate = noise(splits[4], (EXPERTS, D, FF), D ** -0.5, 0.125, ((0, 16),))
    w_up = noise(splits[5], (EXPERTS, D, FF), D ** -0.5, 0.125, ((0, 16),))
    w_down = noise(splits[6], (EXPERTS, FF, D), FF ** -0.5, 0.21875, ((0, 16),))
    return {"tokens": tokens, "out_grad": out_grad, "routes": routes, "probs": probs, "w_gate": w_gate, "w_up": w_up, "w_down": w_down}


def expert_pass(operands):
    x_rows, dy_rows, p_rows, gate_w, up_w, down_w = operands
    x_wide = x_rows.astype(jnp.float32)
    dy_wide = dy_rows.astype(jnp.float32)
    p_wide = p_rows.astype(jnp.float32)
    gate_w32 = gate_w.astype(jnp.float32)
    up_w32 = up_w.astype(jnp.float32)
    down_w32 = down_w.astype(jnp.float32)
    gate = jnp.dot(x_wide, gate_w32)
    up = jnp.dot(x_wide, up_w32)
    sigma = jax.nn.sigmoid(gate)
    hidden = (gate * sigma * up).astype(jnp.bfloat16)
    hidden_wide = hidden.astype(jnp.float32)
    expert_out = jnp.dot(hidden_wide, down_w32)
    pair_grad = jnp.sum(expert_out * dy_wide, axis=1).astype(jnp.bfloat16)
    back = jnp.dot(dy_wide, down_w32.T)
    hidden_grad = p_wide[:, None] * back
    gate_grad = (hidden_grad * up * sigma * (1.0 + gate * (1.0 - sigma))).astype(jnp.bfloat16)
    up_grad = (hidden_grad * gate * sigma).astype(jnp.bfloat16)
    row_grad = jnp.dot(gate_grad.astype(jnp.float32), gate_w32.T) + jnp.dot(up_grad.astype(jnp.float32), up_w32.T)
    scaled = (p_wide[:, None] * dy_wide).astype(jnp.bfloat16)
    down_part = jnp.dot(hidden_wide.T, scaled.astype(jnp.float32)).astype(jnp.bfloat16)
    return row_grad.astype(jnp.bfloat16), pair_grad, down_part


def reference(tokens, out_grad, routes, probs, w_gate, w_up, w_down):
    pair_total = TOKENS * TOPK
    expert_ids = routes.reshape(pair_total).astype(jnp.int32)
    one_hot = (expert_ids[:, None] == jnp.arange(EXPERTS, dtype=jnp.int32)[None, :]).astype(jnp.int32)
    by_source = one_hot.reshape(N_EXPERT, TOK_DEV * TOPK, EXPERTS)
    earlier = jnp.cumsum(by_source, axis=1) - by_source
    slot_ids = jnp.sum(earlier * by_source, axis=2).reshape(pair_total).astype(jnp.int32)
    source_ids = (jnp.arange(pair_total, dtype=jnp.int32) // (TOK_DEV * TOPK)).astype(jnp.int32)
    buffer_row = (source_ids * SLOT + slot_ids).astype(jnp.int32)
    table = jnp.full((EXPERTS, N_EXPERT * SLOT), pair_total, jnp.int32)
    table = table.at[expert_ids, buffer_row].set(jnp.arange(pair_total, dtype=jnp.int32))
    token_of = (table // TOPK).astype(jnp.int32)
    x_padded = jnp.concatenate([tokens, jnp.zeros((1, D), tokens.dtype)], axis=0)
    dy_padded = jnp.concatenate([out_grad, jnp.zeros((1, D), out_grad.dtype)], axis=0)
    p_padded = jnp.concatenate([probs.reshape(pair_total), jnp.zeros((1,), probs.dtype)], axis=0)
    x_rows = x_padded[token_of]
    dy_rows = dy_padded[token_of]
    p_rows = p_padded[table]
    row_grad, pair_grad, down_grad = lax.map(expert_pass, (x_rows, dy_rows, p_rows, w_gate, w_up, w_down))
    summed = jnp.zeros((TOKENS + 1, D), jnp.float32).at[token_of].add(row_grad.astype(jnp.float32))
    input_grad = summed[:TOKENS].astype(jnp.bfloat16)
    pair_values = jnp.zeros((pair_total + 1,), jnp.bfloat16).at[table].set(pair_grad)
    prob_grad = pair_values[:pair_total].reshape(TOKENS, TOPK)
    return input_grad, prob_grad, down_grad
```

```python
import jax
import jax.numpy as jnp
from jax import lax
from jax.sharding import PartitionSpec as P


def body(tokens, out_grad, routes, probs, w_gate, w_up, w_down):
    me = lax.axis_index("expert")
    devices = lax.axis_size("expert")
    tok_count, width = tokens.shape
    gate_w, up_w, down_w = w_gate[0], w_up[0], w_down[0]
    f32, bf16 = jnp.float32, jnp.bfloat16
    experts = jnp.arange(devices, dtype=jnp.int32)
    chosen = routes[:, :, None] == experts[None, None, :]
    dense_p = jnp.sum(jnp.where(chosen, probs.astype(f32)[:, :, None], 0.0), axis=1).astype(bf16)
    x = lax.all_gather(tokens, "expert", axis=0, tiled=True)
    dy = lax.all_gather(out_grad, "expert", axis=0, tiled=True)
    p_all = lax.all_gather(dense_p, "expert", axis=0, tiled=True)
    p = jnp.sum(jnp.where(experts[None, :] == me, p_all.astype(f32), 0.0), axis=1)[:, None]
    gate = jnp.dot(x, gate_w, preferred_element_type=f32)
    up = jnp.dot(x, up_w, preferred_element_type=f32)
    sigma = jax.nn.sigmoid(gate)
    hidden = (gate * sigma * up).astype(bf16)
    back = jnp.einsum("rd,fd->rf", dy, down_w, preferred_element_type=f32)
    pair_grad = jnp.sum(back * hidden.astype(f32), axis=1).astype(bf16)
    hidden_grad = p * back
    gate_grad = (hidden_grad * up * sigma * (1.0 + gate * (1.0 - sigma))).astype(bf16)
    up_grad = (hidden_grad * gate * sigma).astype(bf16)
    row_grad = jnp.einsum("rf,df->rd", gate_grad, gate_w, preferred_element_type=f32)
    row_grad = row_grad + jnp.einsum("rf,df->rd", up_grad, up_w, preferred_element_type=f32)
    input_grad = lax.psum_scatter(
        row_grad.astype(bf16), "expert", scatter_dimension=0, tiled=True
    )
    pairs = lax.all_to_all(
        pair_grad.reshape(devices, tok_count), "expert", split_axis=0, concat_axis=0, tiled=True
    )
    scaled = (p * dy.astype(f32)).astype(bf16)
    down = jnp.einsum("rf,rd->fd", hidden, scaled, preferred_element_type=f32)
    prob_grad = jnp.sum(
        jnp.where(chosen, pairs.T.astype(f32)[:, None, :], 0.0), axis=2
    ).astype(bf16)
    return input_grad, prob_grad, down.astype(bf16)[None]


def solution(mesh):
    rows = P(("groups", "expert"), None)
    slab = P("expert", None, None)
    return jax.shard_map(
        body,
        mesh=mesh,
        in_specs=(rows, rows, rows, rows, slab, slab, slab),
        out_specs=(rows, rows, P(("groups", "expert"), None, None)),
        check_vma=False,
    )
```

```python
import functools

import jax
import jax.numpy as jnp
from jax import lax
from jax.experimental import pallas as pl
from jax.experimental.pallas import tpu as pltpu
from jax.sharding import PartitionSpec as P

F32, BF16 = jnp.float32, jnp.bfloat16
LANES = 128


def place_of(chip, chips):
    odd = chip % 2
    return (1 - odd) * (chip // 2) + odd * (chips - 1 - chip // 2)


def chip_at(place, chips):
    upper = place // (chips // 2)
    return (1 - upper) * (2 * place) + upper * (2 * (chips - 1 - place) + 1)


def kernel(
    devices,
    tok_ref,
    dy_ref,
    routes_ref,
    probs_ref,
    gate_hbm,
    up_hbm,
    down_hbm,
    out_ref,
    prob_ref,
    dgrad_hbm,
    gate_w,
    up_w,
    down_w,
    x_buf,
    d_buf,
    r_buf,
    p_buf,
    a_buf,
    hid_t,
    scaled_buf,
    gg_buf,
    ug_buf,
    dgrad_buf,
    w_sem,
    x_send,
    x_recv,
    d_send,
    d_recv,
    xs_send,
    xs_recv,
    ds_send,
    ds_recv,
    g_send,
    g_recv,
    a_send,
    a_recv,
    o_sem,
):
    chips = devices // 2
    half = chips // 2
    last = half - 1
    rows, width = tok_ref.shape
    top = routes_ref.shape[1]
    hidden_size = gate_w.shape[1]
    mid = rows // 2
    me = lax.axis_index("expert")
    core = me % 2
    chip = me // 2
    place = place_of(chip, chips)
    ahead = chip_at((place + 1) % chips, chips) * 2 + core
    behind = chip_at((place + chips - 1) % chips, chips) * 2 + core
    partner = chip * 2 + (1 - core)

    weights = [
        pltpu.make_async_copy(src, dst, w_sem.at[i])
        for i, (src, dst) in enumerate(((gate_hbm, gate_w), (up_hbm, up_w), (down_hbm, down_w)))
    ]
    barrier = pltpu.get_barrier_semaphore()
    for other in (ahead, behind, partner):
        pl.semaphore_signal(
            barrier, inc=1, device_id={"expert": other}, device_id_type=pl.DeviceIdType.MESH
        )

    lane = lax.broadcasted_iota(jnp.int32, (rows, LANES), 1)
    routes = routes_ref[...]
    probs = probs_ref[...].astype(F32)
    dense_p = jnp.zeros((rows, LANES), F32)
    for k in range(top):
        dense_p = jnp.where(lane == routes[:, k : k + 1], probs[:, k : k + 1], dense_p)
    x_buf[last, 2] = tok_ref[...]
    d_buf[last, 2, :, :width] = dy_ref[...]
    d_buf[last, 2, :, width:] = dense_p.astype(BF16)
    pl.semaphore_wait(barrier, 3)

    def remote(src, dst, send, recv, other):
        return pltpu.make_async_remote_copy(
            src_ref=src,
            dst_ref=dst,
            send_sem=send,
            recv_sem=recv,
            device_id={"expert": other},
            device_id_type=pl.DeviceIdType.MESH,
        )

    def ring(buf, send, recv, src_step, src_way, dst_step, way):
        return remote(
            buf.at[src_step, src_way],
            buf.at[dst_step, 2 * way],
            send.at[dst_step, way],
            recv.at[dst_step, way],
            (ahead, behind)[way],
        )

    def ring_far(buf, send, recv, way):
        part = pl.ds(way * mid, mid)
        return remote(
            buf.at[last - 1, 2 * way, part],
            buf.at[last, 0, part],
            send.at[last, way],
            recv.at[last, way],
            (ahead, behind)[way],
        )

    def swap(buf, send, recv, step, way):
        return remote(
            buf.at[step, 2 * way],
            buf.at[step, 2 * way + 1],
            send.at[step, way],
            recv.at[step, way],
            partner,
        )

    def hand(step, way):
        return remote(
            r_buf.at[step, 2 * way + 1],
            p_buf.at[step, way],
            g_send.at[step, way],
            g_recv.at[step, way],
            partner,
        )

    def back_copy(step, way):
        return remote(
            r_buf.at[step - 1, 2 * way],
            a_buf.at[step - 1, way],
            a_send.at[step - 1, way],
            a_recv.at[step - 1, way],
            (behind, ahead)[way],
        )

    def back_far(way):
        part = pl.ds(way * mid, mid)
        return remote(
            r_buf.at[last, 0, part],
            a_buf.at[last, way, part],
            a_send.at[last, way],
            a_recv.at[last, way],
            (behind, ahead)[way],
        )

    sets = ((x_buf, x_send, x_recv, xs_send, xs_recv), (d_buf, d_send, d_recv, ds_send, ds_recv))

    for buf, send, recv, s_send, s_recv in sets:
        for way in range(2):
            ring(buf, send, recv, last, 2, 0, way).start()
    for copy in weights:
        copy.start()
    for buf, send, recv, s_send, s_recv in sets:
        swap(buf, s_send, s_recv, last, 1).start()

    f_tile = 256
    d_tile = 512
    step_rows = 4 * rows

    def compute(step):
        x = x_buf[step].reshape(step_rows, width)
        dy = d_buf[step, :, :, :width].reshape(step_rows, width)
        p_lanes = d_buf[step, :, :, width:].reshape(step_rows, LANES).astype(F32)
        wide_lane = lax.broadcasted_iota(jnp.int32, (step_rows, LANES), 1)
        mine = wide_lane == me
        p = jnp.sum(jnp.where(mine, p_lanes, 0.0), axis=1, keepdims=True)
        scaled_buf[pl.ds(pl.multiple_of(step * step_rows, step_rows), step_rows), :] = (
            p * dy.astype(F32)
        ).astype(BF16)
        pair = jnp.zeros((step_rows, 1), F32)
        for j in range(hidden_size // f_tile):
            cols = slice(j * f_tile, (j + 1) * f_tile)
            gate = jnp.dot(x, gate_w[:, cols], preferred_element_type=F32)
            up = jnp.dot(x, up_w[:, cols], preferred_element_type=F32)
            back = lax.dot_general(
                dy, down_w[cols, :], (((1,), (1,)), ((), ())), preferred_element_type=F32
            )
            sigma = jax.nn.sigmoid(gate)
            silu = gate * sigma
            hidden = (silu * up).astype(BF16)
            hidden_wide = hidden.astype(F32)
            pair = pair + jnp.sum(back * hidden_wide, axis=1, keepdims=True)
            hidden_grad = p * back
            gg_buf[:, cols] = (hidden_grad * up * sigma * (1.0 + gate * (1.0 - sigma))).astype(BF16)
            ug_buf[:, cols] = (hidden_grad * silu).astype(BF16)
            hid_t[cols, pl.ds(pl.multiple_of(step * step_rows, step_rows), step_rows)] = (
                hidden_wide.T.astype(BF16)
            )
        gg = gg_buf[...]
        ug = ug_buf[...]

        @pl.loop(0, width // d_tile)
        def _(j):
            cols = pl.ds(pl.multiple_of(j * d_tile, d_tile), d_tile)
            grad = lax.dot_general(
                gg, gate_w[cols, :], (((1,), (1,)), ((), ())), preferred_element_type=F32
            )
            grad = grad + lax.dot_general(
                ug, up_w[cols, :], (((1,), (1,)), ((), ())), preferred_element_type=F32
            )
            r_buf[step, :, :, cols] = grad.astype(BF16).reshape(4, rows, d_tile)

        r_buf[step, :, :, width:] = (
            jnp.where(mine, pair, 0.0).astype(BF16).reshape(4, rows, LANES)
        )
        for way in range(2):
            hand(step, way).start()

    @pl.loop(0, half - 2)
    def _(step):
        for buf, send, recv, s_send, s_recv in sets:
            for way in range(2):
                ring(buf, send, recv, step, 2 * way, step, way).wait_recv()
                ring(buf, send, recv, step, 2 * way, step + 1, way).start()
                swap(buf, s_send, s_recv, step, way).start()

        @pl.when(step == 0)
        def _():
            for copy in weights:
                copy.wait()

        for buf, send, recv, s_send, s_recv in sets:
            for way in range(2):
                swap(buf, s_send, s_recv, step, way).wait_recv()
        compute(step)

    step = half - 2
    for buf, send, recv, s_send, s_recv in sets:
        for way in range(2):
            ring(buf, send, recv, step, 2 * way, step, way).wait_recv()
            ring_far(buf, send, recv, way).start()
            swap(buf, s_send, s_recv, step, way).start()
    for buf, send, recv, s_send, s_recv in sets:
        for way in range(2):
            swap(buf, s_send, s_recv, step, way).wait_recv()
    compute(step)

    for buf, send, recv, s_send, s_recv in sets:
        for way in range(2):
            ring_far(buf, send, recv, way).wait_recv()
        swap(buf, s_send, s_recv, last, 0).start()
    for buf, send, recv, s_send, s_recv in sets:
        for way in range(2):
            swap(buf, s_send, s_recv, last, way).wait_recv()
    compute(last)

    def down_tile(j):
        cols = pl.ds(pl.multiple_of(j * f_tile, f_tile), f_tile)
        for i in range(width // d_tile):
            across = slice(i * d_tile, (i + 1) * d_tile)
            dgrad_buf[cols, across] = jnp.dot(
                hid_t[cols, :], scaled_buf[:, across], preferred_element_type=F32
            ).astype(BF16)
        pltpu.make_async_copy(dgrad_buf.at[cols], dgrad_hbm.at[cols], o_sem.at[j]).start()

    tiles = hidden_size // f_tile

    def add(step, way):
        return r_buf[step, 2 * way].astype(F32) + p_buf[step, way].astype(F32)

    hand(last, 0).wait_recv()
    r_buf[last, 0] = add(last, 0).astype(BF16)
    for way in range(2):
        back_far(way).start()
    down_tile(0)
    for way in range(2):
        hand(last - 1, way).wait_recv()
        back_far(way).wait_recv()
        near = slice(way * mid, (way + 1) * mid)
        total = add(last - 1, way)
        r_buf[last - 1, 2 * way] = total.astype(BF16)
        r_buf[last - 1, 2 * way, near] = (
            total[near] + a_buf[last, way, near].astype(F32)
        ).astype(BF16)
        back_copy(last, way).start()
    down_tile(1)

    @pl.loop(0, half - 2)
    def _(i):
        step = half - 2 - i
        for way in range(2):
            hand(step - 1, way).wait_recv()
            back_copy(step + 1, way).wait_recv()
            r_buf[step - 1, 2 * way] = (
                add(step - 1, way) + a_buf[step, way].astype(F32)
            ).astype(BF16)
            back_copy(step, way).start()

        @pl.when(i + 2 < tiles)
        def _():
            down_tile(i + 2)

    hand(last, 1).wait_recv()
    for way in range(2):
        back_copy(1, way).wait_recv()
    total = add(last, 1) + a_buf[0, 0].astype(F32) + a_buf[0, 1].astype(F32)
    out_ref[...] = total[:, :width].astype(BF16)
    pairs = total[:, width:]
    result = jnp.zeros((rows, LANES), F32)
    for k in range(top):
        value = jnp.sum(jnp.where(lane == routes[:, k : k + 1], pairs, 0.0), axis=1, keepdims=True)
        result = jnp.where(lane == k, value, result)
    prob_ref[...] = result[:, :top].astype(BF16)

    for buf, send, recv, s_send, s_recv in sets:
        for way in range(2):
            ring(buf, send, recv, last, 2, 0, way).wait_send()
            ring_far(buf, send, recv, way).wait_send()
            swap(buf, s_send, s_recv, last, way).wait_send()
            swap(buf, s_send, s_recv, last - 1, way).wait_send()
    for way in range(2):
        back_far(way).wait_send()
        back_copy(last, way).wait_send()
        hand(last, way).wait_send()
        hand(last - 1, way).wait_send()

    @pl.loop(0, half - 2)
    def _(step):
        for buf, send, recv, s_send, s_recv in sets:
            for way in range(2):
                ring(buf, send, recv, step, 2 * way, step + 1, way).wait_send()
                swap(buf, s_send, s_recv, step, way).wait_send()
        for way in range(2):
            hand(step, way).wait_send()
            back_copy(step + 1, way).wait_send()

    for j in range(tiles):
        cols = pl.ds(j * f_tile, f_tile)
        pltpu.make_async_copy(dgrad_buf.at[cols], dgrad_hbm.at[cols], o_sem.at[j]).wait()


def body(tokens, out_grad, routes, probs, w_gate, w_up, w_down):
    devices = lax.axis_size("expert")
    half = devices // 4
    rows, width = tokens.shape
    hidden_size = w_gate.shape[2]
    wide = width + LANES
    total = half * 4 * rows
    vmem = pl.BlockSpec(memory_space=pltpu.VMEM)
    hbm = pl.BlockSpec(memory_space=pl.ANY)
    pair_sems = pltpu.SemaphoreType.DMA((half, 2))
    out, prob, down = pl.pallas_call(
        functools.partial(kernel, devices),
        out_shape=(
            jax.ShapeDtypeStruct(tokens.shape, BF16),
            jax.ShapeDtypeStruct(probs.shape, BF16),
            jax.ShapeDtypeStruct(w_down.shape[1:], BF16),
        ),
        in_specs=[vmem] * 4 + [hbm] * 3,
        out_specs=(vmem, vmem, hbm),
        scratch_shapes=[
            pltpu.VMEM((width, hidden_size), BF16),
            pltpu.VMEM((width, hidden_size), BF16),
            pltpu.VMEM((hidden_size, width), BF16),
            pltpu.VMEM((half, 4, rows, width), BF16),
            pltpu.VMEM((half, 4, rows, wide), BF16),
            pltpu.VMEM((half, 4, rows, wide), BF16),
            pltpu.VMEM((half, 2, rows, wide), BF16),
            pltpu.VMEM((half, 2, rows, wide), BF16),
            pltpu.VMEM((hidden_size, total), BF16),
            pltpu.VMEM((total, width), BF16),
            pltpu.VMEM((4 * rows, hidden_size), BF16),
            pltpu.VMEM((4 * rows, hidden_size), BF16),
            pltpu.VMEM((hidden_size, width), BF16),
            pltpu.SemaphoreType.DMA((3,)),
        ]
        + [pair_sems] * 12
        + [pltpu.SemaphoreType.DMA((hidden_size // 256,))],
        compiler_params=pltpu.CompilerParams(
            collective_id=0, has_side_effects=True, vmem_limit_bytes=60 * 1024 * 1024
        ),
        cost_estimate=pl.CostEstimate(
            flops=12 * total * width * hidden_size,
            bytes_accessed=8 * width * hidden_size,
            transcendentals=total * hidden_size,
        ),
    )(tokens, out_grad, routes, probs, w_gate[0], w_up[0], w_down[0])
    return out, prob, down[None]


def solution(mesh):
    rows = P(("groups", "expert"), None)
    slab = P("expert", None, None)
    return jax.shard_map(
        body,
        mesh=mesh,
        in_specs=(rows, rows, rows, rows, slab, slab, slab),
        out_specs=(rows, rows, P(("groups", "expert"), None, None)),
        check_vma=False,
    )
```

```python
import functools

import jax
import jax.numpy as jnp
from jax import lax
from jax.experimental import pallas as pl
from jax.experimental.pallas import tpu as pltpu
from jax.sharding import PartitionSpec as P

F32, BF16 = jnp.float32, jnp.bfloat16
LANES = 128


def place_of(chip, chips):
    odd = chip % 2
    return (1 - odd) * (chip // 2) + odd * (chips - 1 - chip // 2)


def chip_at(place, chips):
    upper = place // (chips // 2)
    return (1 - upper) * (2 * place) + upper * (2 * (chips - 1 - place) + 1)


def kernel(
    devices,
    tok_ref,
    dy_ref,
    routes_ref,
    probs_ref,
    gate_hbm,
    up_hbm,
    down_hbm,
    out_ref,
    prob_ref,
    dgrad_hbm,
    gate_w,
    up_w,
    down_w,
    x_buf,
    d_buf,
    r_buf,
    p_buf,
    a_buf,
    hid_t,
    scaled_buf,
    gg_buf,
    ug_buf,
    w_sem,
    x_send,
    x_recv,
    d_send,
    d_recv,
    xs_send,
    xs_recv,
    ds_send,
    ds_recv,
    g_send,
    g_recv,
    a_send,
    a_recv,
    o_sem,
):
    chips = devices // 2
    half = chips // 2
    last = half - 1
    rows, width = tok_ref.shape
    top = routes_ref.shape[0]
    hidden_size = gate_w.shape[1]
    mid = rows // 2
    wide = width + LANES
    splits = (pl.ds(0, width // 2), pl.ds(width // 2, wide - width // 2))
    me = lax.axis_index("expert")
    core = me % 2
    chip = me // 2
    place = place_of(chip, chips)
    ahead = chip_at((place + 1) % chips, chips) * 2 + core
    behind = chip_at((place + chips - 1) % chips, chips) * 2 + core
    partner = chip * 2 + (1 - core)

    weights = [
        pltpu.make_async_copy(src, dst, w_sem.at[i])
        for i, (src, dst) in enumerate(((gate_hbm, gate_w), (up_hbm, up_w), (down_hbm, down_w)))
    ]
    barrier = pltpu.get_barrier_semaphore()
    for other in (ahead, behind, partner):
        pl.semaphore_signal(
            barrier, inc=1, device_id={"expert": other}, device_id_type=pl.DeviceIdType.MESH
        )

    expert = lax.broadcasted_iota(jnp.int32, (LANES, rows), 0)
    routes = routes_ref[...]
    probs = probs_ref[...].astype(F32)
    dense_p = jnp.zeros((LANES, rows), F32)
    for k in range(top):
        dense_p = jnp.where(expert == routes[k : k + 1], probs[k : k + 1], dense_p)
    x_buf[last, 2] = tok_ref[...]
    d_buf[last, 2, :, :width] = dy_ref[...]
    d_buf[last, 2, :, width:] = dense_p.T.astype(BF16)
    pl.semaphore_wait(barrier, 3)

    def remote(src, dst, send, recv, other):
        return pltpu.make_async_remote_copy(
            src_ref=src,
            dst_ref=dst,
            send_sem=send,
            recv_sem=recv,
            device_id={"expert": other},
            device_id_type=pl.DeviceIdType.MESH,
        )

    def ring(buf, send, recv, src_step, src_way, dst_step, way):
        return remote(
            buf.at[src_step, src_way],
            buf.at[dst_step, 2 * way],
            send.at[dst_step, way],
            recv.at[dst_step, way],
            (ahead, behind)[way],
        )

    def ring_far(buf, send, recv, way):
        part = pl.ds(way * mid, mid)
        return remote(
            buf.at[last - 1, 2 * way, part],
            buf.at[last, 0, part],
            send.at[last, way],
            recv.at[last, way],
            (ahead, behind)[way],
        )

    def swap(buf, send, recv, step, way):
        return remote(
            buf.at[step, 2 * way],
            buf.at[step, 2 * way + 1],
            send.at[step, way],
            recv.at[step, way],
            partner,
        )

    def hand(step, way, c):
        return remote(
            r_buf.at[step, 2 * way + 1, :, splits[c]],
            p_buf.at[step, way, :, splits[c]],
            g_send.at[step, way, c],
            g_recv.at[step, way, c],
            partner,
        )

    def back_copy(step, way, c):
        return remote(
            r_buf.at[step - 1, 2 * way, :, splits[c]],
            a_buf.at[step - 1, way, :, splits[c]],
            a_send.at[step - 1, way, c],
            a_recv.at[step - 1, way, c],
            (behind, ahead)[way],
        )

    def back_far(way, c):
        part = pl.ds(way * mid, mid)
        return remote(
            r_buf.at[last, 0, part, splits[c]],
            a_buf.at[last, way, part, splits[c]],
            a_send.at[last, way, c],
            a_recv.at[last, way, c],
            (behind, ahead)[way],
        )

    sets = ((x_buf, x_send, x_recv, xs_send, xs_recv), (d_buf, d_send, d_recv, ds_send, ds_recv))

    for buf, send, recv, s_send, s_recv in sets:
        for way in range(2):
            ring(buf, send, recv, last, 2, 0, way).start()
    for copy in weights:
        copy.start()
    for buf, send, recv, s_send, s_recv in sets:
        swap(buf, s_send, s_recv, last, 1).start()

    f_tile = 256
    d_tile = 512
    step_rows = 4 * rows

    def pair_mask(count):
        return lax.broadcasted_iota(jnp.int32, (count, LANES), 1) == me

    def inner(step, way, ways):
        count = 2 * ways * rows
        parts = pl.ds(2 * way, 2 * ways)
        x = x_buf[step, parts].reshape(count, width)
        dy = d_buf[step, parts, :, :width].reshape(count, width)
        p_lanes = d_buf[step, parts, :, width:].reshape(count, LANES).astype(F32)
        mine = pair_mask(count)
        p = jnp.sum(jnp.where(mine, p_lanes, 0.0), axis=1, keepdims=True)
        start = step * step_rows + 2 * way * rows
        if not isinstance(start, int):
            start = pl.multiple_of(start, step_rows)
        here = pl.ds(start, count)
        scaled_buf[here, :] = (p * dy.astype(F32)).astype(BF16)
        pair = jnp.zeros((count, 1), F32)
        for j in range(hidden_size // f_tile):
            cols = slice(j * f_tile, (j + 1) * f_tile)
            gate = jnp.dot(x, gate_w[:, cols], preferred_element_type=F32)
            up = jnp.dot(x, up_w[:, cols], preferred_element_type=F32)
            back = lax.dot_general(
                dy, down_w[cols, :], (((1,), (1,)), ((), ())), preferred_element_type=F32
            )
            sigma = jax.nn.sigmoid(gate)
            silu = gate * sigma
            hidden_wide = (silu * up).astype(BF16).astype(F32)
            pair = pair + jnp.sum(back * hidden_wide, axis=1, keepdims=True)
            hidden_grad = p * back
            gg_buf[:count, cols] = (
                hidden_grad * up * sigma * (1.0 + gate * (1.0 - sigma))
            ).astype(BF16)
            ug_buf[:count, cols] = (hidden_grad * silu).astype(BF16)
            hid_t[cols, here] = hidden_wide.T.astype(BF16)
        r_buf[step, parts, :, width:] = (
            jnp.where(mine, pair, 0.0).astype(BF16).reshape(2 * ways, rows, LANES)
        )

    def outer(step, way, ways):
        count = 2 * ways * rows
        parts = pl.ds(2 * way, 2 * ways)
        gg = gg_buf[:count]
        ug = ug_buf[:count]
        for c in range(2):
            for j in range(width // d_tile // 2):
                first = c * (width // 2) + j * d_tile
                cols = slice(first, first + d_tile)
                grad = lax.dot_general(
                    gg, gate_w[cols, :], (((1,), (1,)), ((), ())), preferred_element_type=F32
                )
                grad = grad + lax.dot_general(
                    ug, up_w[cols, :], (((1,), (1,)), ((), ())), preferred_element_type=F32
                )
                r_buf[step, parts, :, cols] = grad.astype(BF16).reshape(2 * ways, rows, d_tile)
            for w in range(way, way + ways):
                hand(step, w, c).start()

    @pl.loop(0, last)
    def _(step):
        for buf, send, recv, s_send, s_recv in sets:
            for way in range(2):
                ring(buf, send, recv, step, 2 * way, step, way).wait_recv()

            @pl.when(step < last - 1)
            def _():
                for way in range(2):
                    ring(buf, send, recv, step, 2 * way, step + 1, way).start()

            @pl.when(step == last - 1)
            def _():
                for way in range(2):
                    ring_far(buf, send, recv, way).start()

            for way in range(2):
                swap(buf, s_send, s_recv, step, way).start()

        @pl.when(step == 0)
        def _():
            for copy in weights:
                copy.wait()
            for buf, send, recv, s_send, s_recv in sets:
                swap(buf, s_send, s_recv, last, 1).wait_recv()
            inner(last, 1, 1)
            outer(last, 1, 1)

        @pl.when(step > 0)
        def _():
            outer(step - 1, 0, 2)

        for buf, send, recv, s_send, s_recv in sets:
            for way in range(2):
                swap(buf, s_send, s_recv, step, way).wait_recv()
        inner(step, 0, 2)

    for buf, send, recv, s_send, s_recv in sets:
        for way in range(2):
            ring_far(buf, send, recv, way).wait_recv()
        swap(buf, s_send, s_recv, last, 0).start()
    outer(last - 1, 0, 2)
    for buf, send, recv, s_send, s_recv in sets:
        swap(buf, s_send, s_recv, last, 0).wait_recv()
    inner(last, 0, 1)
    outer(last, 0, 1)

    def down_tile(j):
        cols = pl.ds(pl.multiple_of(j * f_tile, f_tile), f_tile)
        for i in range(width // d_tile):
            across = slice(i * d_tile, (i + 1) * d_tile)
            down_w[cols, across] = jnp.dot(
                hid_t[cols, :], scaled_buf[:, across], preferred_element_type=F32
            ).astype(BF16)
        pltpu.make_async_copy(down_w.at[cols], dgrad_hbm.at[cols], o_sem.at[j]).start()

    tiles = hidden_size // f_tile

    def add(step, way, c):
        return (
            r_buf[step, 2 * way, :, splits[c]].astype(F32)
            + p_buf[step, way, :, splits[c]].astype(F32)
        )

    for c in range(2):
        hand(last, 0, c).wait_recv()
        r_buf[last, 0, :, splits[c]] = add(last, 0, c).astype(BF16)
        for way in range(2):
            back_far(way, c).start()
    down_tile(0)
    for c in range(2):
        for way in range(2):
            hand(last - 1, way, c).wait_recv()
            back_far(way, c).wait_recv()
            total = add(last - 1, way, c)
            near = slice(way * mid, (way + 1) * mid)
            arrived = a_buf[last, way, near, splits[c]].astype(F32)
            joined = total[near] + arrived
            r_buf[last - 1, 2 * way, :, splits[c]] = total.astype(BF16)
            r_buf[last - 1, 2 * way, near, splits[c]] = joined.astype(BF16)
            back_copy(last, way, c).start()
    down_tile(1)

    @pl.loop(0, half - 2)
    def _(i):
        step = half - 2 - i
        for c in range(2):
            for way in range(2):
                hand(step - 1, way, c).wait_recv()
                back_copy(step + 1, way, c).wait_recv()
                r_buf[step - 1, 2 * way, :, splits[c]] = (
                    add(step - 1, way, c) + a_buf[step, way, :, splits[c]].astype(F32)
                ).astype(BF16)
                back_copy(step, way, c).start()

        @pl.when(i + 2 < tiles)
        def _():
            down_tile(i + 2)

    for c in range(2):
        hand(last, 1, c).wait_recv()
        for way in range(2):
            back_copy(1, way, c).wait_recv()
        total = (
            add(last, 1, c)
            + a_buf[0, 0, :, splits[c]].astype(F32)
            + a_buf[0, 1, :, splits[c]].astype(F32)
        )
        first = c * (width // 2)
        out_ref[:, first : first + width // 2] = total[:, : width // 2].astype(BF16)
    pairs = total[:, width // 2 :].T
    prob_ref[...] = jnp.concatenate(
        [
            jnp.sum(jnp.where(expert == routes[k : k + 1], pairs, 0.0), axis=0, keepdims=True)
            for k in range(top)
        ],
        axis=0,
    ).astype(BF16)

    for buf, send, recv, s_send, s_recv in sets:
        for way in range(2):
            ring(buf, send, recv, last, 2, 0, way).wait_send()
            ring_far(buf, send, recv, way).wait_send()
            swap(buf, s_send, s_recv, last, way).wait_send()
            swap(buf, s_send, s_recv, last - 1, way).wait_send()
    for c in range(2):
        for way in range(2):
            back_far(way, c).wait_send()
            back_copy(last, way, c).wait_send()
            hand(last, way, c).wait_send()
            hand(last - 1, way, c).wait_send()

    @pl.loop(0, half - 2)
    def _(step):
        for buf, send, recv, s_send, s_recv in sets:
            for way in range(2):
                ring(buf, send, recv, step, 2 * way, step + 1, way).wait_send()
                swap(buf, s_send, s_recv, step, way).wait_send()
        for c in range(2):
            for way in range(2):
                hand(step, way, c).wait_send()
                back_copy(step + 1, way, c).wait_send()

    for j in range(tiles):
        cols = pl.ds(j * f_tile, f_tile)
        pltpu.make_async_copy(down_w.at[cols], dgrad_hbm.at[cols], o_sem.at[j]).wait()


def finish(out_in, prob_in, down_in, out_ref, prob_ref, down_ref, stage, in_sem, out_sem):
    pieces = in_sem.shape[0]
    depth = down_in.shape[0] // pieces

    def piece(i):
        return pl.ds(i * depth, depth)

    for i in range(pieces):
        pltpu.make_async_copy(down_in.at[piece(i)], stage.at[piece(i)], in_sem.at[i]).start()
    out_ref[...] = out_in[...]
    prob_ref[...] = prob_in[...]
    for i in range(pieces):
        pltpu.make_async_copy(down_in.at[piece(i)], stage.at[piece(i)], in_sem.at[i]).wait()
        pltpu.make_async_copy(stage.at[piece(i)], down_ref.at[piece(i)], out_sem.at[i]).start()
    for i in range(pieces):
        pltpu.make_async_copy(stage.at[piece(i)], down_ref.at[piece(i)], out_sem.at[i]).wait()


def body(tokens, out_grad, routes, probs, w_gate, w_up, w_down):
    devices = lax.axis_size("expert")
    half = devices // 4
    rows, width = tokens.shape
    hidden_size = w_gate.shape[2]
    wide = width + LANES
    total = half * 4 * rows
    vmem = pl.BlockSpec(memory_space=pltpu.VMEM)
    hbm = pl.BlockSpec(memory_space=pl.ANY)
    pair_sems = pltpu.SemaphoreType.DMA((half, 2))
    split_sems = pltpu.SemaphoreType.DMA((half, 2, 2))
    out, prob, down = pl.pallas_call(
        functools.partial(kernel, devices),
        out_shape=(
            jax.ShapeDtypeStruct(tokens.shape, BF16),
            jax.ShapeDtypeStruct(probs.shape[::-1], BF16),
            jax.ShapeDtypeStruct(w_down.shape[1:], BF16),
        ),
        in_specs=[vmem] * 4 + [hbm] * 3,
        out_specs=(vmem, vmem, hbm),
        scratch_shapes=[
            pltpu.VMEM((width, hidden_size), BF16),
            pltpu.VMEM((width, hidden_size), BF16),
            pltpu.VMEM((hidden_size, width), BF16),
            pltpu.VMEM((half, 4, rows, width), BF16),
            pltpu.VMEM((half, 4, rows, wide), BF16),
            pltpu.VMEM((half, 4, rows, wide), BF16),
            pltpu.VMEM((half, 2, rows, wide), BF16),
            pltpu.VMEM((half, 2, rows, wide), BF16),
            pltpu.VMEM((hidden_size, total), BF16),
            pltpu.VMEM((total, width), BF16),
            pltpu.VMEM((4 * rows, hidden_size), BF16),
            pltpu.VMEM((4 * rows, hidden_size), BF16),
            pltpu.SemaphoreType.DMA((3,)),
        ]
        + [pair_sems] * 8
        + [split_sems] * 4
        + [pltpu.SemaphoreType.DMA((hidden_size // 256,))],
        compiler_params=pltpu.CompilerParams(
            collective_id=0, has_side_effects=True, vmem_limit_bytes=60 * 1024 * 1024
        ),
        cost_estimate=pl.CostEstimate(
            flops=12 * total * width * hidden_size,
            bytes_accessed=8 * width * hidden_size,
            transcendentals=total * hidden_size,
        ),
    )(tokens, out_grad, routes.T, probs.T, w_gate[0], w_up[0], w_down[0])
    out, prob, down = pl.pallas_call(
        finish,
        out_shape=tuple(jax.ShapeDtypeStruct(a.shape, a.dtype) for a in (out, prob, down)),
        in_specs=[vmem, vmem, hbm],
        out_specs=(vmem, vmem, hbm),
        scratch_shapes=[
            pltpu.VMEM(down.shape, BF16),
            pltpu.SemaphoreType.DMA((8,)),
            pltpu.SemaphoreType.DMA((8,)),
        ],
        compiler_params=pltpu.CompilerParams(vmem_limit_bytes=16 * 1024 * 1024),
    )(out, prob, down)
    return out, prob.T, down[None]


def solution(mesh):
    rows = P(("groups", "expert"), None)
    slab = P("expert", None, None)
    return jax.shard_map(
        body,
        mesh=mesh,
        in_specs=(rows, rows, rows, rows, slab, slab, slab),
        out_specs=(rows, rows, P(("groups", "expert"), None, None)),
        check_vma=False,
    )
```

```python
import functools

import jax
import jax.numpy as jnp
from jax import lax
from jax.experimental import pallas as pl
from jax.experimental.pallas import tpu as pltpu
from jax.sharding import PartitionSpec as P

F32, BF16 = jnp.float32, jnp.bfloat16
LANES = 128


def place_of(chip, chips):
    odd = chip % 2
    return (1 - odd) * (chip // 2) + odd * (chips - 1 - chip // 2)


def chip_at(place, chips):
    upper = place // (chips // 2)
    return (1 - upper) * (2 * place) + upper * (2 * (chips - 1 - place) + 1)


def kernel(
    devices,
    tok_ref,
    dy_ref,
    routes_ref,
    probs_ref,
    gate_hbm,
    up_hbm,
    down_hbm,
    out_ref,
    prob_ref,
    dgrad_hbm,
    gate_w,
    up_w,
    down_w,
    x_buf,
    d_buf,
    r_buf,
    p_buf,
    a_buf,
    hid_t,
    scaled_buf,
    gg_buf,
    ug_buf,
    w_sem,
    x_send,
    x_recv,
    d_send,
    d_recv,
    xs_send,
    xs_recv,
    ds_send,
    ds_recv,
    g_send,
    g_recv,
    a_send,
    a_recv,
    o_sem,
):
    chips = devices // 2
    half = chips // 2
    last = half - 1
    rows, width = tok_ref.shape
    top = routes_ref.shape[0]
    hidden_size = gate_w.shape[1]
    mid = rows // 2
    wide = width + LANES
    splits = (pl.ds(0, width // 2), pl.ds(width // 2, wide - width // 2))
    me = lax.axis_index("expert")
    core = me % 2
    chip = me // 2
    place = place_of(chip, chips)
    ahead = chip_at((place + 1) % chips, chips) * 2 + core
    behind = chip_at((place + chips - 1) % chips, chips) * 2 + core
    partner = chip * 2 + (1 - core)

    weights = [
        pltpu.make_async_copy(src, dst, w_sem.at[i])
        for i, (src, dst) in enumerate(((gate_hbm, gate_w), (up_hbm, up_w), (down_hbm, down_w)))
    ]
    barrier = pltpu.get_barrier_semaphore()
    for other in (ahead, behind, partner):
        pl.semaphore_signal(
            barrier, inc=1, device_id={"expert": other}, device_id_type=pl.DeviceIdType.MESH
        )

    expert = lax.broadcasted_iota(jnp.int32, (LANES, rows), 0)
    routes = routes_ref[...]
    probs = probs_ref[...].astype(F32)
    dense_p = jnp.zeros((LANES, rows), F32)
    for k in range(top):
        dense_p = jnp.where(expert == routes[k : k + 1], probs[k : k + 1], dense_p)
    x_buf[last, 2] = tok_ref[...]
    d_buf[last, 2, :, :width] = dy_ref[...]
    d_buf[last, 2, :, width:] = dense_p.T.astype(BF16)
    pl.semaphore_wait(barrier, 3)

    def remote(src, dst, send, recv, other):
        return pltpu.make_async_remote_copy(
            src_ref=src,
            dst_ref=dst,
            send_sem=send,
            recv_sem=recv,
            device_id={"expert": other},
            device_id_type=pl.DeviceIdType.MESH,
        )

    def ring(buf, send, recv, src_step, src_way, dst_step, way):
        return remote(
            buf.at[src_step, src_way],
            buf.at[dst_step, 2 * way],
            send.at[dst_step, way],
            recv.at[dst_step, way],
            (ahead, behind)[way],
        )

    def ring_far(buf, send, recv, way):
        part = pl.ds(way * mid, mid)
        return remote(
            buf.at[last - 1, 2 * way, part],
            buf.at[last, 0, part],
            send.at[last, way],
            recv.at[last, way],
            (ahead, behind)[way],
        )

    def swap(buf, send, recv, step, way):
        return remote(
            buf.at[step, 2 * way],
            buf.at[step, 2 * way + 1],
            send.at[step, way],
            recv.at[step, way],
            partner,
        )

    def hand(step, way, c):
        return remote(
            r_buf.at[step, 2 * way + 1, :, splits[c]],
            p_buf.at[step, way, :, splits[c]],
            g_send.at[step, way, c],
            g_recv.at[step, way, c],
            partner,
        )

    def back_copy(step, way, c):
        return remote(
            r_buf.at[step - 1, 2 * way, :, splits[c]],
            a_buf.at[step - 1, way, :, splits[c]],
            a_send.at[step - 1, way, c],
            a_recv.at[step - 1, way, c],
            (behind, ahead)[way],
        )

    def back_far(way, c):
        part = pl.ds(way * mid, mid)
        return remote(
            r_buf.at[last, 0, part, splits[c]],
            a_buf.at[last, way, part, splits[c]],
            a_send.at[last, way, c],
            a_recv.at[last, way, c],
            (behind, ahead)[way],
        )

    sets = ((x_buf, x_send, x_recv, xs_send, xs_recv), (d_buf, d_send, d_recv, ds_send, ds_recv))

    for buf, send, recv, s_send, s_recv in sets:
        for way in range(2):
            ring(buf, send, recv, last, 2, 0, way).start()
    for copy in weights:
        copy.start()
    for buf, send, recv, s_send, s_recv in sets:
        swap(buf, s_send, s_recv, last, 1).start()

    f_tile = 256
    d_tile = 512
    step_rows = 4 * rows

    def pair_mask(count):
        return lax.broadcasted_iota(jnp.int32, (count, LANES), 1) == me

    def inner(step, way, ways):
        count = 2 * ways * rows
        parts = pl.ds(2 * way, 2 * ways)
        x = x_buf[step, parts].reshape(count, width)
        dy = d_buf[step, parts, :, :width].reshape(count, width)
        p_lanes = d_buf[step, parts, :, width:].reshape(count, LANES).astype(F32)
        mine = pair_mask(count)
        p = jnp.sum(jnp.where(mine, p_lanes, 0.0), axis=1, keepdims=True)
        start = step * step_rows + 2 * way * rows
        if not isinstance(start, int):
            start = pl.multiple_of(start, step_rows)
        here = pl.ds(start, count)
        scaled_buf[here, :] = (p * dy.astype(F32)).astype(BF16)
        pair = jnp.zeros((count, 1), F32)
        for j in range(hidden_size // f_tile):
            cols = slice(j * f_tile, (j + 1) * f_tile)
            gate = jnp.dot(x, gate_w[:, cols], preferred_element_type=F32)
            up = jnp.dot(x, up_w[:, cols], preferred_element_type=F32)
            back = lax.dot_general(
                dy, down_w[cols, :], (((1,), (1,)), ((), ())), preferred_element_type=F32
            )
            sigma = jax.nn.sigmoid(gate)
            silu = gate * sigma
            hidden_wide = (silu * up).astype(BF16).astype(F32)
            pair = pair + jnp.sum(back * hidden_wide, axis=1, keepdims=True)
            hidden_grad = p * back
            gg_buf[:count, cols] = (
                hidden_grad * up * sigma * (1.0 + gate * (1.0 - sigma))
            ).astype(BF16)
            ug_buf[:count, cols] = (hidden_grad * silu).astype(BF16)
            hid_t[cols, here] = hidden_wide.T.astype(BF16)
        r_buf[step, parts, :, width:] = (
            jnp.where(mine, pair, 0.0).astype(BF16).reshape(2 * ways, rows, LANES)
        )

    def outer(step, way, ways):
        count = 2 * ways * rows
        parts = pl.ds(2 * way, 2 * ways)
        gg = gg_buf[:count]
        ug = ug_buf[:count]
        for c in range(2):
            for j in range(width // d_tile // 2):
                first = c * (width // 2) + j * d_tile
                cols = slice(first, first + d_tile)
                grad = lax.dot_general(
                    gg, gate_w[cols, :], (((1,), (1,)), ((), ())), preferred_element_type=F32
                )
                grad = grad + lax.dot_general(
                    ug, up_w[cols, :], (((1,), (1,)), ((), ())), preferred_element_type=F32
                )
                r_buf[step, parts, :, cols] = grad.astype(BF16).reshape(2 * ways, rows, d_tile)
            for w in range(way, way + ways):
                hand(step, w, c).start()

    @pl.loop(0, last)
    def _(step):
        for buf, send, recv, s_send, s_recv in sets:
            for way in range(2):
                ring(buf, send, recv, step, 2 * way, step, way).wait_recv()

            @pl.when(step < last - 1)
            def _():
                for way in range(2):
                    ring(buf, send, recv, step, 2 * way, step + 1, way).start()

            @pl.when(step == last - 1)
            def _():
                for way in range(2):
                    ring_far(buf, send, recv, way).start()

            for way in range(2):
                swap(buf, s_send, s_recv, step, way).start()

        @pl.when(step == 0)
        def _():
            for copy in weights:
                copy.wait()
            for buf, send, recv, s_send, s_recv in sets:
                swap(buf, s_send, s_recv, last, 1).wait_recv()
            inner(last, 1, 1)
            outer(last, 1, 1)

        @pl.when(step > 0)
        def _():
            outer(step - 1, 0, 2)

        for buf, send, recv, s_send, s_recv in sets:
            for way in range(2):
                swap(buf, s_send, s_recv, step, way).wait_recv()
        inner(step, 0, 2)

    for buf, send, recv, s_send, s_recv in sets:
        for way in range(2):
            ring_far(buf, send, recv, way).wait_recv()
        swap(buf, s_send, s_recv, last, 0).start()
    outer(last - 1, 0, 2)
    for buf, send, recv, s_send, s_recv in sets:
        swap(buf, s_send, s_recv, last, 0).wait_recv()
    inner(last, 0, 1)
    outer(last, 0, 1)

    def down_tile(j):
        cols = pl.ds(pl.multiple_of(j * f_tile, f_tile), f_tile)
        for i in range(width // d_tile):
            across = slice(i * d_tile, (i + 1) * d_tile)
            down_w[cols, across] = jnp.dot(
                hid_t[cols, :], scaled_buf[:, across], preferred_element_type=F32
            ).astype(BF16)
        pltpu.make_async_copy(down_w.at[cols], dgrad_hbm.at[cols], o_sem.at[j]).start()

    tiles = hidden_size // f_tile

    def add(step, way, c):
        return (
            r_buf[step, 2 * way, :, splits[c]].astype(F32)
            + p_buf[step, way, :, splits[c]].astype(F32)
        )

    for c in range(2):
        hand(last, 0, c).wait_recv()
        r_buf[last, 0, :, splits[c]] = add(last, 0, c).astype(BF16)
        for way in range(2):
            back_far(way, c).start()
    down_tile(0)
    for c in range(2):
        for way in range(2):
            hand(last - 1, way, c).wait_recv()
            back_far(way, c).wait_recv()
            total = add(last - 1, way, c)
            near = slice(way * mid, (way + 1) * mid)
            arrived = a_buf[last, way, near, splits[c]].astype(F32)
            joined = total[near] + arrived
            r_buf[last - 1, 2 * way, :, splits[c]] = total.astype(BF16)
            r_buf[last - 1, 2 * way, near, splits[c]] = joined.astype(BF16)
            back_copy(last, way, c).start()
    down_tile(1)

    @pl.loop(0, half - 2)
    def _(i):
        step = half - 2 - i
        for c in range(2):
            for way in range(2):
                hand(step - 1, way, c).wait_recv()
                back_copy(step + 1, way, c).wait_recv()
                r_buf[step - 1, 2 * way, :, splits[c]] = (
                    add(step - 1, way, c) + a_buf[step, way, :, splits[c]].astype(F32)
                ).astype(BF16)
                back_copy(step, way, c).start()

        @pl.when(i + 2 < tiles)
        def _():
            down_tile(i + 2)

    for c in range(2):
        hand(last, 1, c).wait_recv()
        for way in range(2):
            back_copy(1, way, c).wait_recv()
        total = (
            add(last, 1, c)
            + a_buf[0, 0, :, splits[c]].astype(F32)
            + a_buf[0, 1, :, splits[c]].astype(F32)
        )
        first = c * (width // 2)
        out_ref[:, first : first + width // 2] = total[:, : width // 2].astype(BF16)
    pairs = total[:, width // 2 :].T
    prob_ref[...] = jnp.concatenate(
        [
            jnp.sum(jnp.where(expert == routes[k : k + 1], pairs, 0.0), axis=0, keepdims=True)
            for k in range(top)
        ],
        axis=0,
    ).astype(BF16)

    for buf, send, recv, s_send, s_recv in sets:
        for way in range(2):
            ring(buf, send, recv, last, 2, 0, way).wait_send()
            ring_far(buf, send, recv, way).wait_send()
            swap(buf, s_send, s_recv, last, way).wait_send()
            swap(buf, s_send, s_recv, last - 1, way).wait_send()
    for c in range(2):
        for way in range(2):
            back_far(way, c).wait_send()
            back_copy(last, way, c).wait_send()
            hand(last, way, c).wait_send()
            hand(last - 1, way, c).wait_send()

    @pl.loop(0, half - 2)
    def _(step):
        for buf, send, recv, s_send, s_recv in sets:
            for way in range(2):
                ring(buf, send, recv, step, 2 * way, step + 1, way).wait_send()
                swap(buf, s_send, s_recv, step, way).wait_send()
        for c in range(2):
            for way in range(2):
                hand(step, way, c).wait_send()
                back_copy(step + 1, way, c).wait_send()

    for j in range(tiles):
        cols = pl.ds(j * f_tile, f_tile)
        pltpu.make_async_copy(down_w.at[cols], dgrad_hbm.at[cols], o_sem.at[j]).wait()


def finish(out_in, prob_in, down_in, out_ref, prob_ref, down_ref, stage, in_sem, out_sem):
    pieces = in_sem.shape[0]
    depth = down_in.shape[0] // pieces

    def piece(i):
        return pl.ds(i * depth, depth)

    for i in range(pieces):
        pltpu.make_async_copy(down_in.at[piece(i)], stage.at[piece(i)], in_sem.at[i]).start()
    out_ref[...] = out_in[...]
    prob_ref[...] = prob_in[...]
    for i in range(pieces):
        pltpu.make_async_copy(down_in.at[piece(i)], stage.at[piece(i)], in_sem.at[i]).wait()
        pltpu.make_async_copy(stage.at[piece(i)], down_ref.at[piece(i)], out_sem.at[i]).start()
    for i in range(pieces):
        pltpu.make_async_copy(stage.at[piece(i)], down_ref.at[piece(i)], out_sem.at[i]).wait()


def body(tokens, out_grad, routes, probs, w_gate, w_up, w_down):
    devices = lax.axis_size("expert")
    half = devices // 4
    rows, width = tokens.shape
    hidden_size = w_gate.shape[2]
    wide = width + LANES
    total = half * 4 * rows
    vmem = pl.BlockSpec(memory_space=pltpu.VMEM)
    hbm = pl.BlockSpec(memory_space=pl.ANY)
    pair_sems = pltpu.SemaphoreType.DMA((half, 2))
    split_sems = pltpu.SemaphoreType.DMA((half, 2, 2))
    out, prob, down = pl.pallas_call(
        functools.partial(kernel, devices),
        out_shape=(
            jax.ShapeDtypeStruct(tokens.shape, BF16),
            jax.ShapeDtypeStruct(probs.shape[::-1], BF16),
            jax.ShapeDtypeStruct(w_down.shape[1:], BF16),
        ),
        in_specs=[vmem] * 4 + [hbm] * 3,
        out_specs=(vmem, vmem, hbm),
        scratch_shapes=[
            pltpu.VMEM((width, hidden_size), BF16),
            pltpu.VMEM((width, hidden_size), BF16),
            pltpu.VMEM((hidden_size, width), BF16),
            pltpu.VMEM((half, 4, rows, width), BF16),
            pltpu.VMEM((half, 4, rows, wide), BF16),
            pltpu.VMEM((half, 4, rows, wide), BF16),
            pltpu.VMEM((half, 2, rows, wide), BF16),
            pltpu.VMEM((half, 2, rows, wide), BF16),
            pltpu.VMEM((hidden_size, total), BF16),
            pltpu.VMEM((total, width), BF16),
            pltpu.VMEM((4 * rows, hidden_size), BF16),
            pltpu.VMEM((4 * rows, hidden_size), BF16),
            pltpu.SemaphoreType.DMA((3,)),
        ]
        + [pair_sems] * 8
        + [split_sems] * 4
        + [pltpu.SemaphoreType.DMA((hidden_size // 256,))],
        compiler_params=pltpu.CompilerParams(
            collective_id=0, has_side_effects=True, vmem_limit_bytes=60 * 1024 * 1024
        ),
        cost_estimate=pl.CostEstimate(
            flops=12 * total * width * hidden_size,
            bytes_accessed=8 * width * hidden_size,
            transcendentals=total * hidden_size,
        ),
    )(tokens, out_grad, routes.T, probs.T, w_gate[0], w_up[0], w_down[0])
    out, prob, down = pl.pallas_call(
        finish,
        out_shape=tuple(jax.ShapeDtypeStruct(a.shape, a.dtype) for a in (out, prob, down)),
        in_specs=[vmem, vmem, hbm],
        out_specs=(vmem, vmem, hbm),
        scratch_shapes=[
            pltpu.VMEM(down.shape, BF16),
            pltpu.SemaphoreType.DMA((8,)),
            pltpu.SemaphoreType.DMA((8,)),
        ],
        compiler_params=pltpu.CompilerParams(vmem_limit_bytes=60 * 1024 * 1024),
    )(out, prob, down)
    return out, prob.T, down[None]


def solution(mesh):
    rows = P(("groups", "expert"), None)
    slab = P("expert", None, None)
    return jax.shard_map(
        body,
        mesh=mesh,
        in_specs=(rows, rows, rows, rows, slab, slab, slab),
        out_specs=(rows, rows, P(("groups", "expert"), None, None)),
        check_vma=False,
    )
```
